512 devices in a mesh: cfg: 2 (over core), blk: 32 (over z_lo, y), uly: 8 (over x, z_hi).
Axes of the slice: x: 4, y: 8, z: 8 (z_hi: 2, z_lo: 4; z = z_hi * 4 + z_lo), core: 2. Of those that a mesh axis runs over, the one named last changes fastest.
Arguments:
- hidden: bfloat16 [2, 4608, 3072], P('cfg', ('blk', 'uly')), may hold values from -3 to 3
- qkv: bfloat16 [2, 4608, 3, 3072], P('cfg', ('blk', 'uly')), may hold values from -80 to 80
- step_gate: float32 [2, 28, 3072], P('cfg'), may hold values from -6 to 6
- text_len: int32 [2], P('cfg'), may hold values from 128 to 512, as said below
- step_index: int32 [1], replicated, may hold values from 0 to 27
- guidance: float32 [1], replicated, may hold values from 1.5 to 4.5
- q_gain: float32 [128], replicated, may hold values from 1 to 6
- k_gain: float32 [128], replicated, may hold values from 1 to 6
- out_weight: bfloat16 [3072, 3072], P('uly'), may hold values from -0.109375 to 0.109375
Outputs:
- guided: bfloat16 [4608, 3072], P(('blk', 'uly'), 'cfg')
The draws below stay inside these ranges and needn't reach their ends.
Inputs may be any that keep to these rules, and one draw needn't show every extreme that they name: `text_len`: in every draw at least one branch has all 512 text tokens valid.
All inputs are finite; a program needn't handle non-finite values.
Results may differ from the reference program's by a relative error of at most 0.02.
The reference program's roundings to bfloat16 on the way count: a program that leaves them out, or rounds other values in their place, can miss the bound.
Values may be sent and summed in bfloat16 or wider, within the bound.
A program may use at most 64 MiB of HBM per device.

```python
import math
import jax
import jax.numpy as jnp
from jax import lax

D = 3072
HEADS = 24
HD = 128
TXT = 512
STEPS = 28
SEQ = 4608


def gain_draw(key, lower, upper):
    return jnp.exp(jax.random.uniform(key, (HD,), jnp.float32, math.log(lower), math.log(upper)))


def draw_q_gain(key, part):
    key = jax.random.fold_in(key, 2)
    return gain_draw(key, 1.0, 1.8)


def draw_k_gain(key, part):
    key = jax.random.fold_in(key, 3)
    return gain_draw(key, 1.0, 1.8)


def draw_text_len(key, part):
    key = jax.random.fold_in(key, 1)
    first_key, second_key = jax.random.split(key)
    lengths = jax.random.randint(first_key, (2,), TXT // 4, TXT + 1, dtype=jnp.int32)
    full_branch = jax.random.randint(second_key, (), 0, 2, dtype=jnp.int32)
    slots = jnp.arange(2, dtype=jnp.int32)
    return jnp.where(slots == full_branch, TXT, lengths).astype(jnp.int32)


def draw_qkv(key, part):
    key = jax.random.fold_in(key, 4)
    base_key, row_key, col_key = jax.random.split(key, 3)
    shape = (2, SEQ, 3, D)
    base = jnp.clip(jax.random.normal(base_key, shape, jnp.float32), -4.0, 4.0)
    row_scale = jnp.exp(jax.random.uniform(row_key, (2, SEQ, 3, 1), jnp.float32, 0.0, math.log(10.0)))
    col_scale = jnp.exp(jax.random.uniform(col_key, (1, 1, 3, D), jnp.float32, math.log(0.5), math.log(2.0)))
    drawn = base * row_scale * col_scale
    return jnp.clip(drawn, -80.0, 80.0).astype(jnp.bfloat16)


def steps_of(own_key, extent, cuts, least, high):
    loudness = 1.0
    for position, parts in cuts:
        draws = jax.random.uniform(jax.random.fold_in(jax.random.fold_in(own_key, 6), position), (parts,), jnp.float32, least / len(cuts), high / len(cuts))
        loudness = loudness * jnp.repeat(jnp.exp(draws), extent[position] // parts).reshape((-1,) + (1,) * (len(extent) - 1 - position))
    return loudness


def centred(key, extent, spread, reach, cuts=(), held_as=jnp.bfloat16):
    gain = steps_of(key, extent, cuts, -0.22, 0.18) if cuts else 1.0
    result = jax.random.normal(key, extent, jnp.float32) * spread * gain
    return jnp.minimum(jnp.maximum(result, -reach), reach).astype(held_as)


def setup_inputs(seed: int = 0) -> dict:
    splits = jax.random.split(jax.random.key(seed), 10)
    return {
        "hidden": centred(splits[0], (2, SEQ, D), 0.5, 3.0, ((0, 2), (1, 256))),
        "qkv": draw_qkv(jax.random.fold_in(splits[9], 71), 0),
        "step_gate": centred(splits[2], (2, STEPS, D), 1.5, 6.0, ((0, 2),), jnp.float32),
        "text_len": draw_text_len(jax.random.fold_in(splits[9], 71), 0),
        "step_index": jax.random.randint(splits[4], (1,), 0, STEPS).astype(jnp.int32),
        "guidance": jnp.clip(jax.random.uniform(splits[5], (1,), jnp.float32, 1.5, 4.5), 1.5, 4.5),
        "q_gain": draw_q_gain(jax.random.fold_in(splits[9], 71), 0),
        "k_gain": draw_k_gain(jax.random.fold_in(splits[9], 71), 0),
        "out_weight": centred(splits[8], (D, D), D ** -0.5, 0.109375, ((0, 8),)),
    }


epsilon = 1e-06
masked_score = -1e+30

def norm_heads(source, scale_gain):
    mean_square = lax.optimization_barrier(jnp.mean(source * source, axis=-1, keepdims=True))
    return (source * lax.rsqrt(mean_square + epsilon) * scale_gain).astype(jnp.bfloat16)

def reference(hidden, qkv, step_gate, text_len, step_index, guidance, q_gain, k_gain, out_weight):
    inv_root = 1.0 / math.sqrt(HD)
    positions = jnp.arange(SEQ, dtype=jnp.int32)
    outputs = []
    for branch_id in range(2):
        heads_all = qkv[branch_id].astype(jnp.float32).reshape(SEQ, 3, HEADS, HD)
        q_normed = norm_heads(heads_all[:, 0], q_gain)
        k_normed = norm_heads(heads_all[:, 1], k_gain)
        values = qkv[branch_id, :, 2].reshape(SEQ, HEADS, HD)
        kept_keys = (positions >= TXT) | (positions < text_len[branch_id])

        def one_head(items):
            query_head, key_head, value_head = items
            scores = jnp.dot(query_head, key_head.T, preferred_element_type=jnp.float32) * inv_root
            scores = jnp.where(kept_keys[None, :], scores, masked_score)
            largest = lax.optimization_barrier(jnp.max(scores, axis=-1, keepdims=True))
            weights = jnp.exp(scores - largest)
            total = lax.optimization_barrier(jnp.sum(weights, axis=-1, keepdims=True))
            mixed = jnp.dot(weights.astype(jnp.bfloat16), value_head, preferred_element_type=jnp.float32)
            return (mixed / total).astype(jnp.bfloat16)
        per_head = lax.map(one_head, (jnp.transpose(q_normed, (1, 0, 2)), jnp.transpose(k_normed, (1, 0, 2)), jnp.transpose(values, (1, 0, 2))))
        attn = jnp.transpose(per_head, (1, 0, 2)).reshape(SEQ, D)
        proj = jnp.dot(attn, out_weight, preferred_element_type=jnp.float32)
        gate_row = lax.dynamic_slice_in_dim(step_gate[branch_id], step_index[0], 1, 0)
        outputs.append((hidden[branch_id].astype(jnp.float32) + gate_row * proj).astype(jnp.bfloat16))
    cond = outputs[0].astype(jnp.float32)
    uncond = outputs[1].astype(jnp.float32)
    return (uncond + guidance[0] * (cond - uncond)).astype(jnp.bfloat16)
```

```python
import functools
import math

import jax
import jax.numpy as jnp
from jax import lax
from jax.experimental import pallas as pl
from jax.experimental.pallas import tpu as pltpu
from jax.sharding import PartitionSpec as P

TXT = 512
HEAD = 128
GROUP = 3
TOK = 18
MAIN = 16
TAIL = TOK - MAIN
PIECE = 4 * MAIN
Z_RUN = 4

epsilon = 1e-06
masked_score = -1e30
MESH = pl.DeviceIdType.MESH
f32, bf16 = jnp.float32, jnp.bfloat16


def kernel(
    sizes,
    hidden_hbm,
    qkv_hbm,
    gate_hbm,
    weight_hbm,
    small_ref,
    out_ref,
    hidden_ref,
    qkv_ref,
    gate_ref,
    weight,
    gate_rows,
    send,
    tail32,
    stage,
    queries,
    kv,
    lifts,
    stat,
    acc,
    part_send,
    part_recv,
    stat_send,
    stat_recv,
    attn,
    attn_other,
    early,
    rows32,
    x_send,
    x_recv,
    z_send,
    z_recv,
    hid_send,
    hid_recv,
    gate_send,
    gate_recv,
    load_sem,
    a2a_send_sem,
    a2a_recv_sem,
    q_send_sem,
    q_recv_sem,
    ring_send_sem,
    ring_recv_sem,
    part_send_sem,
    part_recv_sem,
    cross_send_sem,
    cross_recv_sem,
    x_send_sem,
    x_recv_sem,
    z_send_sem,
    z_recv_sem,
):
    n_u, n_y, n_z = sizes
    block = n_u * TOK
    mains = n_u * MAIN
    tile = n_u * TAIL
    width = n_u * GROUP * HEAD
    half = width // 2
    padded = stat.shape[2]
    chunks, pieces = x_send.shape[0], x_send.shape[2]
    strips = (pieces - 1) // 2
    chunk = strips * HEAD
    n_x = n_u // 2
    far = n_y // 2
    c = lax.axis_index("cfg")
    b = lax.axis_index("blk")
    u = lax.axis_index("uly")
    other = 1 - c
    zl = b // n_y
    y = b % n_y
    mirror = n_z - 1 - zl
    x = u // 2
    zh = u % 2
    across = (c, mirror * n_y + y, u + 1 - 2 * zh)
    right = (c, zl * n_y + (y + 1) % n_y, u)
    left = (c, zl * n_y + (y + n_y - 1) % n_y, u)

    def u_peer(d):
        return (u + d) % n_u

    def u_device(d):
        return (c, b if d % 2 == 0 else mirror * n_y + y, u_peer(d))

    def z_peer(d):
        return (zl + d) % n_z

    def z_device(d):
        return (c, z_peer(d) * n_y + y, u)

    barrier = pltpu.get_barrier_semaphore()
    greet = [u_device(d) for d in range(1, n_u)]
    greet += [z_device(d) for d in range(1, n_z)]
    greet += [right, left, (other, b, u)]
    for who in greet:
        pl.semaphore_signal(barrier, inc=1, device_id=who, device_id_type=MESH)

    loads = [
        pltpu.make_async_copy(src, dst, load_sem.at[i])
        for i, (src, dst) in enumerate(
            [
                (qkv_hbm, qkv_ref),
                (hidden_hbm, hidden_ref),
                (gate_hbm, gate_ref),
                (weight_hbm, weight),
            ]
        )
    ]
    for load in loads:
        load.start()

    def remote(src, dst, send_sem, recv_sem, who):
        return pltpu.make_async_remote_copy(
            src_ref=src,
            dst_ref=dst,
            send_sem=send_sem,
            recv_sem=recv_sem,
            device_id=who,
            device_id_type=MESH,
        )

    started = []

    def go(copy):
        copy.start()
        started.append(copy)

    tail32[...] = jnp.zeros_like(tail32)
    pad = padded - n_z * block
    queries[:, n_z * block : padded, :] = jnp.zeros((GROUP, pad, HEAD), bf16)
    stat[...] = jnp.ones_like(stat)
    loads[0].wait()

    def lay_out(h):
        for g in range(n_u):
            col = (g * GROUP + h) * HEAD
            for part in range(3):
                rows = qkv_ref[:, part, col : col + HEAD].astype(f32)
                if part < 2:
                    gain = small_ref[part : part + 1, :]
                    mean_square = jnp.mean(rows * rows, axis=-1, keepdims=True)
                    rows = rows * lax.rsqrt(mean_square + epsilon) * gain
                send[h, g, MAIN * part : MAIN * (part + 1), :] = rows[:MAIN].astype(bf16)
                tail32[h, g, TAIL * part : TAIL * (part + 1), :] = rows[MAIN:]
        for g in range(n_u):
            send[h, g, 3 * MAIN :, :] = tail32[h, g].astype(bf16)

    def a2a_copy(h, d):
        return remote(
            send.at[h, u_peer(d)],
            stage.at[h, u],
            a2a_send_sem.at[h, d],
            a2a_recv_sem.at[h, n_u - d],
            u_device(d),
        )

    def a2a_wait(h, d):
        remote(
            send.at[h, u_peer(d)],
            stage.at[h, u_peer(d)],
            a2a_send_sem.at[h, d],
            a2a_recv_sem.at[h, d],
            u_device(d),
        ).wait_recv()

    for h in range(GROUP):
        lay_out(h)
        if h == 0:
            pl.semaphore_wait(barrier, len(greet))
        for d in range(1, n_u):
            go(a2a_copy(h, d))
        stage[h, u] = send[h, u]

    def cross_copy(i, src, dst):
        return remote(src, dst, cross_send_sem.at[i], cross_recv_sem.at[i], (other, b, u))

    def half_columns(side):
        return pl.ds(pl.multiple_of(side * half, 128), half)

    loads[1].wait()
    loads[2].wait()
    hid_send[...] = jnp.zeros_like(hid_send)
    hid_send[0:TOK, :] = hidden_ref[:, half_columns(other)]
    step = small_ref[3:4, 0:1]
    gate_rows[...] = functools.reduce(
        jnp.add, [jnp.where(step == float(i), gate_ref[i], 0.0) for i in range(gate_ref.shape[0])]
    )
    gate_send[...] = jnp.broadcast_to(gate_rows[:, half_columns(other)], gate_send.shape)
    hid_copy = cross_copy(GROUP, hid_send, hid_recv)
    gate_copy = cross_copy(GROUP + 1, gate_send, gate_recv)
    go(hid_copy)
    go(gate_copy)

    row = lax.broadcasted_iota(jnp.int32, (block, 1), 0)
    late = row - mains
    source = jnp.where(row < mains, row // MAIN, late // TAIL)
    within = jnp.where(row < mains, row % MAIN, MAIN + late % TAIL)
    source_z = jnp.where(source % 2 == u % 2, zl, mirror)
    token = source_z * (n_y * block) + source * TOK + within
    text_limit = small_ref[2:3, 0:1]
    for slot in range(n_y):
        position = token + slot * block
        kept = (position >= TXT) | (position.astype(f32) < text_limit)
        lifts[slot] = jnp.where(kept, 0.0, masked_score)

    to = lax.broadcasted_iota(jnp.int32, (3 * tile, n_u * MAIN), 0)
    of = lax.broadcasted_iota(jnp.int32, (3 * tile, n_u * MAIN), 1)
    wanted = MAIN * ((to % tile) // TAIL) + TAIL * (to // tile) + to % TAIL
    pick = jnp.where(of == wanted, 1.0, 0.0).astype(bf16)

    def query_rows(h, z):
        return queries.at[h, pl.ds(pl.multiple_of(block * z, MAIN), block), :]

    def assemble(h):
        for d in range(1, n_u):
            a2a_wait(h, d)
        tails = stage[h, :, 3 * MAIN :, :].reshape(n_u * MAIN, HEAD)
        fixed = jnp.dot(pick, tails, preferred_element_type=f32).astype(bf16)
        for part in range(2):
            rows = stage[h, :, MAIN * (part + 1) : MAIN * (part + 2), :]
            kv[y, h, part, :mains, :] = rows.reshape(mains, HEAD)
            kv[y, h, part, mains:, :] = fixed[tile * (part + 1) : tile * (part + 2)]
        ring_step(h, 1)
        main_rows = pl.ds(pl.multiple_of(block * zl, MAIN), mains)
        tail_rows = pl.ds(pl.multiple_of(block * zl + mains, MAIN), tile)
        queries[h, main_rows, :] = stage[h, :, 0:MAIN, :].reshape(mains, HEAD)
        queries[h, tail_rows, :] = fixed[:tile]
        for d in range(1, n_z):
            go(
                remote(
                    query_rows(h, zl),
                    query_rows(h, zl),
                    q_send_sem.at[h, d],
                    q_recv_sem.at[h, n_z - d],
                    z_device(d),
                )
            )

    def await_queries(h):
        for d in range(1, n_z):
            rows = query_rows(h, z_peer(d))
            remote(rows, rows, q_send_sem.at[h, d], q_recv_sem.at[h, d], z_device(d)).wait_recv()

    def behind(s):
        return (y - s + n_y) % n_y

    def ahead(s):
        return (y + s) % n_y

    def ring_piece(h, s, way, slot):
        piece = kv.at[slot, h] if s < far else kv.at[slot, h, way]
        return remote(
            piece,
            piece,
            ring_send_sem.at[h, s, way],
            ring_recv_sem.at[h, s, way],
            right if way == 0 else left,
        )

    def ring_wait(h, s):
        for way in range(2):
            ring_piece(h, s, way, behind(s) if way == 0 else ahead(s)).wait_recv()

    def ring_step(h, s):
        for way in range(2):
            if s > 1:
                slot = behind(s - 1) if way == 0 else ahead(s - 1)
                ring_piece(h, s - 1, way, slot).wait_recv()
            go(ring_piece(h, s, way, behind(s - 1) if way == 0 else ahead(s - 1)))

    factor = math.log2(math.e) / math.sqrt(HEAD)
    rows_rows = (((1,), (1,)), ((), ()))
    first_first = (((0,), (0,)), ((), ()))

    def attend(h, slots, first=False):
        keys = jnp.concatenate([kv[slot, h, 0] for slot in slots], axis=0)
        values = jnp.concatenate([kv[slot, h, 1] for slot in slots], axis=0)
        lift = jnp.concatenate([lifts[slot] for slot in slots], axis=0)
        scores = (
            lax.dot_general(keys, queries[h], rows_rows, preferred_element_type=f32) + lift
        )
        top = jnp.max(scores, axis=0, keepdims=True)
        if not first:
            before = stat[h, 0:1, :]
            top = jnp.maximum(top, before)
            shrink = jnp.exp2((before - top) * factor)
        weights = jnp.exp2((scores - top) * factor)
        summed = jnp.sum(weights, axis=0, keepdims=True)
        mixed = lax.dot_general(
            values, weights.astype(bf16), first_first, preferred_element_type=f32
        )
        stat[h, 0:1, :] = top
        if first:
            stat[h, 1:2, :] = summed
            acc[h] = mixed
        else:
            stat[h, 1:2, :] = stat[h, 1:2, :] * shrink + summed
            acc[h] = acc[h] * shrink + mixed

    def part_copies(h, d, i, z, mine, theirs):
        return [
            remote(
                stat_send.at[h, z],
                stat_recv.at[h, i],
                part_send_sem.at[h, 0, d],
                part_recv_sem.at[h, 0, theirs],
                z_device(d),
            ),
            remote(
                part_send.at[h, z],
                part_recv.at[h, i],
                part_send_sem.at[h, 1, d],
                part_recv_sem.at[h, 1, theirs],
                z_device(d),
            ),
        ]

    def hand_back(h):
        stats = stat[h]
        for i in range(n_z):
            moved = stats if i == 0 else pltpu.roll(stats, padded - block * i, 1)
            stat_send[h, i] = jnp.concatenate([moved[0:4, :128], moved[0:4, 128:256]], axis=0)
        turned = jnp.transpose(acc[h]).astype(bf16)
        for i in range(n_z):
            part_send[h, i] = turned[block * i : block * (i + 1)]
        for d in range(1, n_z):
            for copy in part_copies(h, d, n_z - d - 1, z_peer(d), d, n_z - d):
                go(copy)

    def combine(h):
        for d in range(1, n_z):
            for copy in part_copies(h, d, d - 1, z_peer(d), d, d):
                copy.wait_recv()
        held = [stat_send[h, zl]] + [stat_recv[h, d] for d in range(n_z - 1)]
        top = functools.reduce(jnp.maximum, held)
        shares = [jnp.exp2((s - top) * factor) for s in held]
        lines = []
        for at in (0, 4):
            whole = sum(w[at : at + 1] * s[at + 1 : at + 2] for w, s in zip(shares, held))
            lines += [w[at : at + 1] / whole for w in shares]
        columns = jnp.transpose(jnp.concatenate(lines, axis=0))
        terms = [part_send[h, zl]] + [part_recv[h, d] for d in range(n_z - 1)]
        early_rows = sum(t[:128].astype(f32) * columns[:, k : k + 1] for k, t in enumerate(terms))
        late_rows = sum(
            t[128:].astype(f32) * columns[: block - 128, n_z + k : n_z + k + 1]
            for k, t in enumerate(terms)
        )
        attn[h, :128, :] = early_rows.astype(bf16)
        attn[h, 128:, :] = late_rows.astype(bf16)
        copy = cross_copy(h, attn.at[h], attn_other.at[h])
        go(copy)
        return copy

    assemble(0)
    assemble(1)
    ring_step(0, 2)
    await_queries(0)
    attend(0, [y, behind(1), ahead(1)], first=True)
    assemble(2)
    ring_step(0, 3)
    ring_step(1, 2)
    attend(0, [behind(2), ahead(2)])
    await_queries(1)
    attend(1, [y, behind(1), ahead(1)], first=True)
    ring_step(0, 4)
    ring_step(1, 3)
    ring_step(2, 2)
    attend(1, [behind(2), ahead(2)])
    await_queries(2)
    attend(2, [y, behind(1), ahead(1)], first=True)
    ring_wait(0, far)
    attend(0, [behind(3), ahead(3), ahead(far)])
    hand_back(0)
    ring_step(1, 4)
    ring_step(2, 3)
    attend(2, [behind(2), ahead(2)])
    ring_wait(1, far)
    attend(1, [behind(3), ahead(3), ahead(far)])
    hand_back(1)
    ring_step(2, 4)
    attend(2, [behind(3), ahead(3)])
    ring_wait(2, far)
    attend(2, [ahead(far)])
    settled = len(started)
    hand_back(2)

    guide = small_ref[4:5, 0:1]
    coefficient = jnp.where(c == 0, guide, 1.0 - guide)
    crossed = [combine(h) for h in range(GROUP - 1)]
    loads[3].wait()
    gate_copy.wait_recv()
    for copy in crossed:
        copy.wait_recv()
    done = HEAD * (GROUP - 1)

    def project(n, rows, own, others):
        at = pl.ds(pl.multiple_of(c * half + chunk * n, 128), chunk)
        cols = slice(chunk * n, chunk * (n + 1))
        scale = gate_rows[:, at] * coefficient
        scale_other = gate_recv[0:1, cols] * (1.0 - coefficient)
        part = weight[rows, at]
        return (
            jnp.dot(own, part, preferred_element_type=f32) * scale
            + jnp.dot(others, part, preferred_element_type=f32) * scale_other
        )

    first_own = jnp.concatenate([attn[h] for h in range(GROUP - 1)], axis=1)
    first_other = jnp.concatenate([attn_other[h] for h in range(GROUP - 1)], axis=1)
    for n in range(chunks):
        early[n] = project(n, slice(0, done), first_own, first_other)
    hid_copy.wait_recv()
    kept_hidden = hidden_ref[:, half_columns(c)].astype(f32)
    residual = kept_hidden * coefficient + hid_recv[0:TOK, :].astype(f32) * (1.0 - coefficient)
    for copy in started[:settled]:
        copy.wait_send()
    combine(GROUP - 1).wait_recv()

    def x_copy(n, d, i, theirs):
        there = (x + d) % n_x
        return remote(
            x_send.at[n, there],
            x_recv.at[n, i],
            x_send_sem.at[n, d],
            x_recv_sem.at[n, theirs],
            (c, b, 2 * there + zh),
        )

    def z_copy(n):
        return remote(z_send.at[n], z_recv.at[n], z_send_sem.at[n], z_recv_sem.at[n], across)

    last_own, last_other = attn[GROUP - 1], attn_other[GROUP - 1]
    for n in range(chunks):
        summed = early[n] + project(n, slice(done, done + HEAD), last_own, last_other)
        for i in range(strips):
            strip = summed[:, HEAD * i : HEAD * (i + 1)]
            for j in range(n_u):
                rows32[n, j // 2, (j % 2) * strips + i] = strip[MAIN * j : MAIN * (j + 1)]
            for j in range(n_x):
                rows32[n, j, 2 * strips, 2 * TAIL * i : 2 * TAIL * (i + 1), :] = strip[
                    mains + 2 * TAIL * j : mains + 2 * TAIL * (j + 1)
                ]
        x_send[n] = rows32[n].astype(bf16)
        for d in range(1, n_x):
            go(x_copy(n, d, n_x - d - 1, n_x - d))

    sums = []
    for n in range(chunks):
        for d in range(1, n_x):
            x_copy(n, d, d - 1, d).wait_recv()
        summed = rows32[n, x]
        for d in range(1, n_x):
            summed += x_recv[n, d - 1].astype(f32)
        is_low = zh == 0
        here = jnp.where(is_low, summed[:strips], summed[strips : 2 * strips])
        there = jnp.where(is_low, summed[strips : 2 * strips], summed[:strips])
        z_send[n, :strips] = there.astype(bf16)
        z_send[n, strips] = summed[2 * strips].astype(bf16)
        go(z_copy(n))
        sums.append((here, summed[2 * strips]))
    for n in range(chunks):
        z_copy(n).wait_recv()
        here, tail = sums[n]
        tail = tail + z_recv[n, strips].astype(f32)
        for i in range(strips):
            cols = slice(chunk * n + HEAD * i, chunk * n + HEAD * (i + 1))
            main_rows = here[i] + z_recv[n, i].astype(f32)
            at = 2 * TAIL * i
            tail_rows = jnp.where(is_low, tail[at : at + TAIL], tail[at + TAIL : at + 2 * TAIL])
            out_ref[0:MAIN, cols] = (residual[0:MAIN, cols] + main_rows).astype(bf16)
            out_ref[MAIN:TOK, cols] = (residual[MAIN:TOK, cols] + tail_rows).astype(bf16)
    for copy in started[settled:]:
        copy.wait_send()


def on_device(sizes, hidden, qkv, step_gate, text_len, step_index, guidance, q_gain, k_gain, out_weight):
    n_u, n_y, n_z = sizes
    block = n_u * TOK
    width = n_u * GROUP * HEAD
    half = width // 2
    chunks = 3
    chunk = half // chunks
    strips = chunk // HEAD
    pieces = 2 * strips + 1
    n_x = n_u // 2
    padded = -(-n_z * block // 128) * 128
    far = n_y // 2
    steps = step_gate.shape[1]
    vmem, dma = pltpu.VMEM, pltpu.SemaphoreType.DMA
    in_hbm = pl.BlockSpec(memory_space=pltpu.HBM)
    row = lax.broadcasted_iota(jnp.int32, (8, HEAD), 0)
    small = jnp.where(row == 0, q_gain[None, :], k_gain[None, :])
    for at, scalar in ((2, text_len), (3, step_index), (4, guidance)):
        small = jnp.where(row == at, scalar.astype(f32), small)
    return pl.pallas_call(
        functools.partial(kernel, sizes),
        out_shape=jax.ShapeDtypeStruct((TOK, half), bf16),
        in_specs=[in_hbm] * 4 + [pl.BlockSpec(memory_space=vmem)],
        out_specs=pl.BlockSpec(memory_space=vmem),
        scratch_shapes=[
            vmem((TOK, width), bf16),
            vmem((TOK, 3, width), bf16),
            vmem((steps, 1, width), f32),
            vmem((GROUP * HEAD, width), bf16),
            vmem((1, width), f32),
            vmem((GROUP, n_u, PIECE, HEAD), bf16),
            vmem((GROUP, n_u, MAIN, HEAD), f32),
            vmem((GROUP, n_u, PIECE, HEAD), bf16),
            vmem((GROUP, padded, HEAD), bf16),
            vmem((n_y, GROUP, 2, block, HEAD), bf16),
            vmem((n_y, block, 1), f32),
            vmem((GROUP, 8, padded), f32),
            vmem((GROUP, HEAD, padded), f32),
            vmem((GROUP, n_z, block, HEAD), bf16),
            vmem((GROUP, n_z - 1, block, HEAD), bf16),
            vmem((GROUP, n_z, 8, 128), f32),
            vmem((GROUP, n_z - 1, 8, 128), f32),
            vmem((GROUP, block, HEAD), bf16),
            vmem((GROUP, block, HEAD), bf16),
            vmem((chunks, block, chunk), f32),
            vmem((chunks, n_x, pieces, MAIN, HEAD), f32),
            vmem((chunks, n_x, pieces, MAIN, HEAD), bf16),
            vmem((chunks, n_x - 1, pieces, MAIN, HEAD), bf16),
            vmem((chunks, strips + 1, MAIN, HEAD), bf16),
            vmem((chunks, strips + 1, MAIN, HEAD), bf16),
            vmem((32, half), bf16),
            vmem((32, half), bf16),
            vmem((8, half), f32),
            vmem((8, half), f32),
            dma((4,)),
            dma((GROUP, n_u)),
            dma((GROUP, n_u)),
            dma((GROUP, n_z)),
            dma((GROUP, n_z)),
            dma((GROUP, far + 1, 2)),
            dma((GROUP, far + 1, 2)),
            dma((GROUP, 2, n_z)),
            dma((GROUP, 2, n_z)),
            dma((GROUP + 2,)),
            dma((GROUP + 2,)),
            dma((chunks, n_x)),
            dma((chunks, n_x)),
            dma((chunks,)),
            dma((chunks,)),
        ],
        compiler_params=pltpu.CompilerParams(
            collective_id=0, has_side_effects=True, vmem_limit_bytes=55104 * 1024
        ),
        cost_estimate=pl.CostEstimate(
            flops=2 * n_z * n_y * block * block * GROUP * HEAD * 2,
            bytes_accessed=8 * 1024 * 1024,
            transcendentals=n_z * n_y * block * block * GROUP,
        ),
    )(
        hidden[0],
        qkv[0],
        jnp.transpose(step_gate, (1, 0, 2)),
        out_weight,
        small,
    )


def solution(mesh):
    placed = (
        P("cfg", ("blk", "uly"), None),
        P("cfg", ("blk", "uly"), None, None),
        P("cfg", None, None),
        P("cfg"),
        P(),
        P(),
        P(),
        P(),
        P("uly", None),
    )
    sizes = (mesh.shape["uly"], mesh.shape["blk"] // Z_RUN, Z_RUN)
    return jax.shard_map(
        functools.partial(on_device, sizes),
        mesh=mesh,
        in_specs=placed,
        out_specs=P(("blk", "uly"), "cfg"),
        check_vma=False,
    )
```

```python
import functools
import math

import jax
import jax.numpy as jnp
from jax import lax
from jax.experimental import pallas as pl
from jax.experimental.pallas import tpu as pltpu
from jax.sharding import PartitionSpec as P

TXT = 512
HEAD = 128
GROUP = 3
TOK = 18
MAIN = 16
TAIL = TOK - MAIN
PIECE = 4 * MAIN
Z_RUN = 4

epsilon = 1e-06
masked_score = -1e30
MESH = pl.DeviceIdType.MESH
f32, bf16 = jnp.float32, jnp.bfloat16


def kernel(
    sizes,
    hidden_hbm,
    qkv_hbm,
    gate_hbm,
    weight_hbm,
    small_ref,
    out_ref,
    hidden_ref,
    qkv_ref,
    gate_ref,
    weight,
    gate_rows,
    send,
    tail32,
    stage,
    queries,
    kv,
    lifts,
    stat,
    acc,
    part_send,
    part_recv,
    stat_send,
    stat_recv,
    attn,
    attn_other,
    early,
    rows32,
    x_send,
    x_recv,
    z_send,
    z_recv,
    hid_send,
    hid_recv,
    gate_send,
    gate_recv,
    load_sem,
    a2a_send_sem,
    a2a_recv_sem,
    q_send_sem,
    q_recv_sem,
    ring_send_sem,
    ring_recv_sem,
    part_send_sem,
    part_recv_sem,
    cross_send_sem,
    cross_recv_sem,
    x_send_sem,
    x_recv_sem,
    z_send_sem,
    z_recv_sem,
):
    n_u, n_y, n_z = sizes
    block = n_u * TOK
    mains = n_u * MAIN
    tile = n_u * TAIL
    width = n_u * GROUP * HEAD
    half = width // 2
    padded = stat.shape[2]
    chunks, pieces = x_send.shape[0], x_send.shape[2]
    strips = (pieces - 1) // 2
    chunk = strips * HEAD
    n_x = n_u // 2
    far = n_y // 2
    c = lax.axis_index("cfg")
    b = lax.axis_index("blk")
    u = lax.axis_index("uly")
    other = 1 - c
    zl = b // n_y
    y = b % n_y
    mirror = n_z - 1 - zl
    x = u // 2
    zh = u % 2
    across = (c, mirror * n_y + y, u + 1 - 2 * zh)
    right = (c, zl * n_y + (y + 1) % n_y, u)
    left = (c, zl * n_y + (y + n_y - 1) % n_y, u)
    right_two = (c, zl * n_y + (y + 2) % n_y, u)
    left_two = (c, zl * n_y + (y + n_y - 2) % n_y, u)

    def u_peer(d):
        return (u + d) % n_u

    def u_device(d):
        return (c, b if d % 2 == 0 else mirror * n_y + y, u_peer(d))

    def z_peer(d):
        return (zl + d) % n_z

    def z_device(d):
        return (c, z_peer(d) * n_y + y, u)

    barrier = pltpu.get_barrier_semaphore()
    greet = [u_device(d) for d in range(1, n_u)]
    greet += [z_device(d) for d in range(1, n_z)]
    greet += [right_two, left_two]
    greet += [right, left, (other, b, u)]
    for who in greet:
        pl.semaphore_signal(barrier, inc=1, device_id=who, device_id_type=MESH)

    loads = [
        pltpu.make_async_copy(src, dst, load_sem.at[i])
        for i, (src, dst) in enumerate(
            [
                (qkv_hbm, qkv_ref),
                (hidden_hbm, hidden_ref),
                (gate_hbm, gate_ref),
                (weight_hbm, weight),
            ]
        )
    ]
    for load in loads:
        load.start()

    def remote(src, dst, send_sem, recv_sem, who):
        return pltpu.make_async_remote_copy(
            src_ref=src,
            dst_ref=dst,
            send_sem=send_sem,
            recv_sem=recv_sem,
            device_id=who,
            device_id_type=MESH,
        )

    started = []

    def go(copy):
        copy.start()
        started.append(copy)

    tail32[...] = jnp.zeros_like(tail32)
    pad = padded - n_z * block
    queries[:, n_z * block : padded, :] = jnp.zeros((GROUP, pad, HEAD), bf16)
    stat[...] = jnp.ones_like(stat)
    loads[0].wait()

    def lay_out(h):
        for g in range(n_u):
            col = (g * GROUP + h) * HEAD
            for part in range(3):
                rows = qkv_ref[:, part, col : col + HEAD].astype(f32)
                if part < 2:
                    gain = small_ref[part : part + 1, :]
                    mean_square = jnp.mean(rows * rows, axis=-1, keepdims=True)
                    rows = rows * lax.rsqrt(mean_square + epsilon) * gain
                send[h, g, MAIN * part : MAIN * (part + 1), :] = rows[:MAIN].astype(bf16)
                tail32[h, g, TAIL * part : TAIL * (part + 1), :] = rows[MAIN:]
        for g in range(n_u):
            send[h, g, 3 * MAIN :, :] = tail32[h, g].astype(bf16)

    def a2a_copy(h, d):
        return remote(
            send.at[h, u_peer(d)],
            stage.at[h, u],
            a2a_send_sem.at[h, d],
            a2a_recv_sem.at[h, n_u - d],
            u_device(d),
        )

    def a2a_wait(h, d):
        remote(
            send.at[h, u_peer(d)],
            stage.at[h, u_peer(d)],
            a2a_send_sem.at[h, d],
            a2a_recv_sem.at[h, d],
            u_device(d),
        ).wait_recv()

    for h in range(GROUP):
        lay_out(h)
        if h == 0:
            pl.semaphore_wait(barrier, len(greet))
        for d in range(1, n_u):
            go(a2a_copy(h, d))
        stage[h, u] = send[h, u]

    def cross_copy(i, src, dst):
        return remote(src, dst, cross_send_sem.at[i], cross_recv_sem.at[i], (other, b, u))

    def half_columns(side):
        return pl.ds(pl.multiple_of(side * half, 128), half)

    loads[1].wait()
    loads[2].wait()
    hid_send[...] = jnp.zeros_like(hid_send)
    hid_send[0:TOK, :] = hidden_ref[:, half_columns(other)]
    step = small_ref[3:4, 0:1]
    gate_rows[...] = functools.reduce(
        jnp.add, [jnp.where(step == float(i), gate_ref[i], 0.0) for i in range(gate_ref.shape[0])]
    )
    gate_send[...] = jnp.broadcast_to(gate_rows[:, half_columns(other)], gate_send.shape)
    hid_copy = cross_copy(GROUP, hid_send, hid_recv)
    gate_copy = cross_copy(GROUP + 1, gate_send, gate_recv)
    go(hid_copy)
    go(gate_copy)

    row = lax.broadcasted_iota(jnp.int32, (block, 1), 0)
    late = row - mains
    source = jnp.where(row < mains, row // MAIN, late // TAIL)
    within = jnp.where(row < mains, row % MAIN, MAIN + late % TAIL)
    source_z = jnp.where(source % 2 == u % 2, zl, mirror)
    token = source_z * (n_y * block) + source * TOK + within
    text_limit = small_ref[2:3, 0:1]
    for slot in range(n_y):
        position = token + slot * block
        kept = (position >= TXT) | (position.astype(f32) < text_limit)
        lifts[slot] = jnp.where(kept, 0.0, masked_score)

    to = lax.broadcasted_iota(jnp.int32, (3 * tile, n_u * MAIN), 0)
    of = lax.broadcasted_iota(jnp.int32, (3 * tile, n_u * MAIN), 1)
    wanted = MAIN * ((to % tile) // TAIL) + TAIL * (to // tile) + to % TAIL
    pick = jnp.where(of == wanted, 1.0, 0.0).astype(bf16)

    def query_rows(h, z):
        return queries.at[h, pl.ds(pl.multiple_of(block * z, MAIN), block), :]

    def assemble(h):
        for d in range(1, n_u):
            a2a_wait(h, d)
        tails = stage[h, :, 3 * MAIN :, :].reshape(n_u * MAIN, HEAD)
        fixed = jnp.dot(pick, tails, preferred_element_type=f32).astype(bf16)
        for part in range(2):
            rows = stage[h, :, MAIN * (part + 1) : MAIN * (part + 2), :]
            kv[y, h, part, :mains, :] = rows.reshape(mains, HEAD)
            kv[y, h, part, mains:, :] = fixed[tile * (part + 1) : tile * (part + 2)]
        ring_step(h, 1)
        main_rows = pl.ds(pl.multiple_of(block * zl, MAIN), mains)
        tail_rows = pl.ds(pl.multiple_of(block * zl + mains, MAIN), tile)
        queries[h, main_rows, :] = stage[h, :, 0:MAIN, :].reshape(mains, HEAD)
        queries[h, tail_rows, :] = fixed[:tile]
        for d in range(1, n_z):
            go(
                remote(
                    query_rows(h, zl),
                    query_rows(h, zl),
                    q_send_sem.at[h, d],
                    q_recv_sem.at[h, n_z - d],
                    z_device(d),
                )
            )

    def await_queries(h):
        for d in range(1, n_z):
            rows = query_rows(h, z_peer(d))
            remote(rows, rows, q_send_sem.at[h, d], q_recv_sem.at[h, d], z_device(d)).wait_recv()

    def behind(s):
        return (y - s + n_y) % n_y

    def ahead(s):
        return (y + s) % n_y

    def ring_piece(h, s, way, slot):
        piece = kv.at[slot, h] if s < far else kv.at[slot, h, way]
        return remote(
            piece,
            piece,
            ring_send_sem.at[h, s, way],
            ring_recv_sem.at[h, s, way],
            right if way == 0 else left,
        )

    def ring_leap(h):
        for way in range(2):
            piece = kv.at[behind(far - 2) if way == 0 else ahead(far - 2), h, way]
            go(
                remote(
                    piece,
                    piece,
                    ring_send_sem.at[h, far, way],
                    ring_recv_sem.at[h, far, way],
                    right_two if way == 0 else left_two,
                )
            )

    def ring_wait(h, s):
        for way in range(2):
            ring_piece(h, s, way, behind(s) if way == 0 else ahead(s)).wait_recv()

    def ring_step(h, s):
        for way in range(2):
            if s > 1:
                slot = behind(s - 1) if way == 0 else ahead(s - 1)
                ring_piece(h, s - 1, way, slot).wait_recv()
            go(ring_piece(h, s, way, behind(s - 1) if way == 0 else ahead(s - 1)))

    factor = math.log2(math.e) / math.sqrt(HEAD)
    rows_rows = (((1,), (1,)), ((), ()))
    first_first = (((0,), (0,)), ((), ()))

    def attend(h, slots, first=False):
        keys = jnp.concatenate([kv[slot, h, 0] for slot in slots], axis=0)
        values = jnp.concatenate([kv[slot, h, 1] for slot in slots], axis=0)
        lift = jnp.concatenate([lifts[slot] for slot in slots], axis=0)
        scores = (
            lax.dot_general(keys, queries[h], rows_rows, preferred_element_type=f32) + lift
        )
        top = jnp.max(scores, axis=0, keepdims=True)
        if not first:
            before = stat[h, 0:1, :]
            top = jnp.maximum(top, before)
            shrink = jnp.exp2((before - top) * factor)
        weights = jnp.exp2((scores - top) * factor)
        summed = jnp.sum(weights, axis=0, keepdims=True)
        mixed = lax.dot_general(
            values, weights.astype(bf16), first_first, preferred_element_type=f32
        )
        stat[h, 0:1, :] = top
        if first:
            stat[h, 1:2, :] = summed
            acc[h] = mixed
        else:
            stat[h, 1:2, :] = stat[h, 1:2, :] * shrink + summed
            acc[h] = acc[h] * shrink + mixed

    def part_copies(h, d, i, z, mine, theirs):
        return [
            remote(
                stat_send.at[h, z],
                stat_recv.at[h, i],
                part_send_sem.at[h, 0, d],
                part_recv_sem.at[h, 0, theirs],
                z_device(d),
            ),
            remote(
                part_send.at[h, z],
                part_recv.at[h, i],
                part_send_sem.at[h, 1, d],
                part_recv_sem.at[h, 1, theirs],
                z_device(d),
            ),
        ]

    def hand_back(h):
        stats = stat[h]
        for i in range(n_z):
            moved = stats if i == 0 else pltpu.roll(stats, padded - block * i, 1)
            stat_send[h, i] = jnp.concatenate([moved[0:4, :128], moved[0:4, 128:256]], axis=0)
        turned = jnp.transpose(acc[h]).astype(bf16)
        for i in range(n_z):
            part_send[h, i] = turned[block * i : block * (i + 1)]
        for d in range(1, n_z):
            for copy in part_copies(h, d, n_z - d - 1, z_peer(d), d, n_z - d):
                go(copy)

    def combine(h):
        for d in range(1, n_z):
            for copy in part_copies(h, d, d - 1, z_peer(d), d, d):
                copy.wait_recv()
        held = [stat_send[h, zl]] + [stat_recv[h, d] for d in range(n_z - 1)]
        top = functools.reduce(jnp.maximum, held)
        shares = [jnp.exp2((s - top) * factor) for s in held]
        lines = []
        for at in (0, 4):
            whole = sum(w[at : at + 1] * s[at + 1 : at + 2] for w, s in zip(shares, held))
            lines += [w[at : at + 1] / whole for w in shares]
        columns = jnp.transpose(jnp.concatenate(lines, axis=0))
        terms = [part_send[h, zl]] + [part_recv[h, d] for d in range(n_z - 1)]
        early_rows = sum(t[:128].astype(f32) * columns[:, k : k + 1] for k, t in enumerate(terms))
        late_rows = sum(
            t[128:].astype(f32) * columns[: block - 128, n_z + k : n_z + k + 1]
            for k, t in enumerate(terms)
        )
        attn[h, :128, :] = early_rows.astype(bf16)
        attn[h, 128:, :] = late_rows.astype(bf16)
        copy = cross_copy(h, attn.at[h], attn_other.at[h])
        go(copy)
        return copy

    assemble(0)
    assemble(1)
    ring_step(0, 2)
    await_queries(0)
    attend(0, [y, behind(1), ahead(1)], first=True)
    assemble(2)
    ring_step(0, 3)
    ring_step(1, 2)
    attend(0, [behind(2), ahead(2)])
    await_queries(1)
    attend(1, [y, behind(1), ahead(1)], first=True)
    ring_step(0, 4)
    ring_step(1, 3)
    ring_step(2, 2)
    attend(1, [behind(2), ahead(2)])
    await_queries(2)
    attend(2, [y, behind(1), ahead(1)], first=True)
    ring_wait(0, far)
    ring_step(1, 4)
    ring_step(2, 3)
    ring_leap(2)
    attend(0, [behind(3), ahead(3), ahead(far)])
    hand_back(0)
    attend(2, [behind(2), ahead(2)])
    ring_wait(1, far)
    attend(1, [behind(3), ahead(3), ahead(far)])
    hand_back(1)
    ring_wait(2, 3)
    ring_wait(2, far)
    attend(2, [behind(3), ahead(3), ahead(far)])
    settled = len(started)
    hand_back(2)

    guide = small_ref[4:5, 0:1]
    coefficient = jnp.where(c == 0, guide, 1.0 - guide)
    crossed = [combine(h) for h in range(GROUP - 1)]
    loads[3].wait()
    gate_copy.wait_recv()
    for copy in crossed:
        copy.wait_recv()
    done = HEAD * (GROUP - 1)

    def project(n, rows, own, others):
        at = pl.ds(pl.multiple_of(c * half + chunk * n, 128), chunk)
        cols = slice(chunk * n, chunk * (n + 1))
        scale = gate_rows[:, at] * coefficient
        scale_other = gate_recv[0:1, cols] * (1.0 - coefficient)
        part = weight[rows, at]
        return (
            jnp.dot(own, part, preferred_element_type=f32) * scale
            + jnp.dot(others, part, preferred_element_type=f32) * scale_other
        )

    first_own = jnp.concatenate([attn[h] for h in range(GROUP - 1)], axis=1)
    first_other = jnp.concatenate([attn_other[h] for h in range(GROUP - 1)], axis=1)
    for n in range(chunks):
        early[n] = project(n, slice(0, done), first_own, first_other)
    hid_copy.wait_recv()
    kept_hidden = hidden_ref[:, half_columns(c)].astype(f32)
    residual = kept_hidden * coefficient + hid_recv[0:TOK, :].astype(f32) * (1.0 - coefficient)
    for copy in started[:settled]:
        copy.wait_send()
    combine(GROUP - 1).wait_recv()

    def x_copy(n, d, i, theirs):
        there = (x + d) % n_x
        return remote(
            x_send.at[n, there],
            x_recv.at[n, i],
            x_send_sem.at[n, d],
            x_recv_sem.at[n, theirs],
            (c, b, 2 * there + zh),
        )

    def z_copy(n):
        return remote(z_send.at[n], z_recv.at[n], z_send_sem.at[n], z_recv_sem.at[n], across)

    last_own, last_other = attn[GROUP - 1], attn_other[GROUP - 1]
    for n in range(chunks):
        summed = early[n] + project(n, slice(done, done + HEAD), last_own, last_other)
        for i in range(strips):
            strip = summed[:, HEAD * i : HEAD * (i + 1)]
            for j in range(n_u):
                rows32[n, j // 2, (j % 2) * strips + i] = strip[MAIN * j : MAIN * (j + 1)]
            for j in range(n_x):
                rows32[n, j, 2 * strips, 2 * TAIL * i : 2 * TAIL * (i + 1), :] = strip[
                    mains + 2 * TAIL * j : mains + 2 * TAIL * (j + 1)
                ]
        x_send[n] = rows32[n].astype(bf16)
        for d in range(1, n_x):
            go(x_copy(n, d, n_x - d - 1, n_x - d))

    sums = []
    for n in range(chunks):
        for d in range(1, n_x):
            x_copy(n, d, d - 1, d).wait_recv()
        summed = rows32[n, x]
        for d in range(1, n_x):
            summed += x_recv[n, d - 1].astype(f32)
        is_low = zh == 0
        here = jnp.where(is_low, summed[:strips], summed[strips : 2 * strips])
        there = jnp.where(is_low, summed[strips : 2 * strips], summed[:strips])
        z_send[n, :strips] = there.astype(bf16)
        z_send[n, strips] = summed[2 * strips].astype(bf16)
        go(z_copy(n))
        sums.append((here, summed[2 * strips]))
    for n in range(chunks):
        z_copy(n).wait_recv()
        here, tail = sums[n]
        tail = tail + z_recv[n, strips].astype(f32)
        for i in range(strips):
            cols = slice(chunk * n + HEAD * i, chunk * n + HEAD * (i + 1))
            main_rows = here[i] + z_recv[n, i].astype(f32)
            at = 2 * TAIL * i
            tail_rows = jnp.where(is_low, tail[at : at + TAIL], tail[at + TAIL : at + 2 * TAIL])
            out_ref[0:MAIN, cols] = (residual[0:MAIN, cols] + main_rows).astype(bf16)
            out_ref[MAIN:TOK, cols] = (residual[MAIN:TOK, cols] + tail_rows).astype(bf16)
    for copy in started[settled:]:
        copy.wait_send()


def on_device(sizes, hidden, qkv, step_gate, text_len, step_index, guidance, q_gain, k_gain, out_weight):
    n_u, n_y, n_z = sizes
    block = n_u * TOK
    width = n_u * GROUP * HEAD
    half = width // 2
    chunks = 3
    chunk = half // chunks
    strips = chunk // HEAD
    pieces = 2 * strips + 1
    n_x = n_u // 2
    padded = -(-n_z * block // 128) * 128
    far = n_y // 2
    steps = step_gate.shape[1]
    vmem, dma = pltpu.VMEM, pltpu.SemaphoreType.DMA
    in_hbm = pl.BlockSpec(memory_space=pltpu.HBM)
    row = lax.broadcasted_iota(jnp.int32, (8, HEAD), 0)
    small = jnp.where(row == 0, q_gain[None, :], k_gain[None, :])
    for at, scalar in ((2, text_len), (3, step_index), (4, guidance)):
        small = jnp.where(row == at, scalar.astype(f32), small)
    return pl.pallas_call(
        functools.partial(kernel, sizes),
        out_shape=jax.ShapeDtypeStruct((TOK, half), bf16),
        in_specs=[in_hbm] * 4 + [pl.BlockSpec(memory_space=vmem)],
        out_specs=pl.BlockSpec(memory_space=vmem),
        scratch_shapes=[
            vmem((TOK, width), bf16),
            vmem((TOK, 3, width), bf16),
            vmem((steps, 1, width), f32),
            vmem((GROUP * HEAD, width), bf16),
            vmem((1, width), f32),
            vmem((GROUP, n_u, PIECE, HEAD), bf16),
            vmem((GROUP, n_u, MAIN, HEAD), f32),
            vmem((GROUP, n_u, PIECE, HEAD), bf16),
            vmem((GROUP, padded, HEAD), bf16),
            vmem((n_y, GROUP, 2, block, HEAD), bf16),
            vmem((n_y, block, 1), f32),
            vmem((GROUP, 8, padded), f32),
            vmem((GROUP, HEAD, padded), f32),
            vmem((GROUP, n_z, block, HEAD), bf16),
            vmem((GROUP, n_z - 1, block, HEAD), bf16),
            vmem((GROUP, n_z, 8, 128), f32),
            vmem((GROUP, n_z - 1, 8, 128), f32),
            vmem((GROUP, block, HEAD), bf16),
            vmem((GROUP, block, HEAD), bf16),
            vmem((chunks, block, chunk), f32),
            vmem((chunks, n_x, pieces, MAIN, HEAD), f32),
            vmem((chunks, n_x, pieces, MAIN, HEAD), bf16),
            vmem((chunks, n_x - 1, pieces, MAIN, HEAD), bf16),
            vmem((chunks, strips + 1, MAIN, HEAD), bf16),
            vmem((chunks, strips + 1, MAIN, HEAD), bf16),
            vmem((32, half), bf16),
            vmem((32, half), bf16),
            vmem((8, half), f32),
            vmem((8, half), f32),
            dma((4,)),
            dma((GROUP, n_u)),
            dma((GROUP, n_u)),
            dma((GROUP, n_z)),
            dma((GROUP, n_z)),
            dma((GROUP, far + 1, 2)),
            dma((GROUP, far + 1, 2)),
            dma((GROUP, 2, n_z)),
            dma((GROUP, 2, n_z)),
            dma((GROUP + 2,)),
            dma((GROUP + 2,)),
            dma((chunks, n_x)),
            dma((chunks, n_x)),
            dma((chunks,)),
            dma((chunks,)),
        ],
        compiler_params=pltpu.CompilerParams(
            collective_id=0, has_side_effects=True, vmem_limit_bytes=55104 * 1024
        ),
        cost_estimate=pl.CostEstimate(
            flops=2 * n_z * n_y * block * block * GROUP * HEAD * 2,
            bytes_accessed=8 * 1024 * 1024,
            transcendentals=n_z * n_y * block * block * GROUP,
        ),
    )(
        hidden[0],
        qkv[0],
        jnp.transpose(step_gate, (1, 0, 2)),
        out_weight,
        small,
    )


def solution(mesh):
    placed = (
        P("cfg", ("blk", "uly"), None),
        P("cfg", ("blk", "uly"), None, None),
        P("cfg", None, None),
        P("cfg"),
        P(),
        P(),
        P(),
        P(),
        P("uly", None),
    )
    sizes = (mesh.shape["uly"], mesh.shape["blk"] // Z_RUN, Z_RUN)
    return jax.shard_map(
        functools.partial(on_device, sizes),
        mesh=mesh,
        in_specs=placed,
        out_specs=P(("blk", "uly"), "cfg"),
        check_vma=False,
    )
```
